32 devices in a mesh: ctx: 16 (over z, y, x), head: 2 (over core).
Axes of the slice: x: 2, y: 2, z: 4, core: 2. Of those that a mesh axis runs over, the one named last changes fastest.
Arguments:
- query: bfloat16 [6144, 6144], P(('ctx', 'head')), may hold values from -6 to 6
- key_in: bfloat16 [6144, 6144], P(('ctx', 'head')), may hold values from -6 to 6
- value: bfloat16 [6144, 6144], P(('ctx', 'head')), may hold values from -6 to 6
- cotangent: bfloat16 [6144, 6144], P(('ctx', 'head')), may hold values from -18 to 18
- decay_rate: float32 [48, 16], replicated, as said below
- residue: float32 [48, 16], replicated, may hold values from -2 to 2
Outputs:
- mixed: bfloat16 [6144, 6144], P(('ctx', 'head'))
- grad_query: bfloat16 [6144, 6144], P(('ctx', 'head'))
- grad_key: bfloat16 [6144, 6144], P(('ctx', 'head'))
- grad_value: bfloat16 [6144, 6144], P(('ctx', 'head'))
- residue_grad: float32 [48, 16], P('head')
The draws below stay inside these ranges and needn't reach their ends.
Inputs may be any that keep to these rules, and one draw needn't show every extreme that they name: `decay_rate`: positive decay rates of at most 1/30.
All inputs are finite; a program needn't handle non-finite values.
Results may differ from the reference program's by a relative error of at most 0.00105.
Values may be sent and summed in bfloat16 or wider, within the bound.
A program may use at most 192 MiB of HBM per device.

```python
import math
import jax
import jax.numpy as jnp
from jax import lax

HEADS = 48
HEAD_DIM = 128
POLES = 16
D = 6144
LEN = 6144


def draw_decay_rate(key, part):
    flag_key, level_key = jax.random.split(key)
    slow_share = 0.5
    slow_head = jax.random.uniform(flag_key, (HEADS, 1), jnp.float32) < slow_share
    level_draw = jax.random.uniform(level_key, (HEADS, POLES), jnp.float32)
    slow_low = math.log(0.2 / LEN)
    slow_high = math.log(2.0 / LEN)
    fast_low = math.log(2.0 / LEN)
    fast_high = math.log(1.0 / 30.0)
    slow_rates = jnp.exp(slow_low + level_draw * (slow_high - slow_low))
    fast_rates = jnp.exp(fast_low + level_draw * (fast_high - fast_low))
    return jnp.where(slow_head, slow_rates, fast_rates).astype(jnp.float32)


def draw_cotangent(key, part):
    position = jnp.arange(LEN, dtype=jnp.float32) / max(LEN - 1, 1)
    envelope = 1.0 + 2.0 * position
    base_draw = jnp.clip(jax.random.normal(key, (LEN, HEADS * HEAD_DIM), jnp.float32), -6.0, 6.0)
    return (base_draw * envelope[:, None]).astype(jnp.bfloat16)


def shard_levels(stream_key, shape, cuts, least, high):
    loudness = 1.0
    for dim, blocks in cuts:
        heights = jax.random.uniform(jax.random.fold_in(jax.random.fold_in(stream_key, 6), dim), (blocks,), jnp.float32, least / len(cuts), high / len(cuts))
        loudness = loudness * jnp.repeat(jnp.exp(heights), shape[dim] // blocks).reshape((-1,) + (1,) * (len(shape) - 1 - dim))
    return loudness


def gaussian(own_key, shape, scale, most, cuts=(), kind=jnp.bfloat16):
    factor_of = shard_levels(own_key, shape, cuts, -0.22, 0.18) if cuts else 1.0
    array = jax.random.normal(own_key, shape, jnp.float32) * scale * factor_of
    return jnp.minimum(jnp.maximum(array, -most), most).astype(kind)


def setup_inputs(seed: int = 0) -> dict:
    arg_keys = jax.random.split(jax.random.key(seed), 7)
    return {
        "query": gaussian(arg_keys[0], (LEN, D), 1.0, 6.0, ((0, 32),)),
        "key_in": gaussian(arg_keys[1], (LEN, D), 1.0, 6.0, ((0, 32),)),
        "value": gaussian(arg_keys[2], (LEN, D), 1.0, 6.0, ((0, 32),)),
        "cotangent": draw_cotangent(jax.random.fold_in(arg_keys[6], 71), 0),
        "decay_rate": draw_decay_rate(jax.random.fold_in(arg_keys[6], 71), 0),
        "residue": gaussian(arg_keys[5], (HEADS, POLES), 0.35, 2.0, (), jnp.float32),
    }


def reference(query, key_in, value, cotangent, decay_rate, residue):
    norm_factor = jnp.sqrt(-jnp.expm1(-2.0 * decay_rate))
    coefficient = residue * norm_factor
    positions = jnp.arange(LEN, dtype=jnp.float32)
    fft_length = 2 * LEN

    def head_terms(head_index):
        first_col = (head_index * HEAD_DIM).astype(jnp.int32)

        def columns(source):
            return lax.dynamic_slice_in_dim(source, first_col, HEAD_DIM, 1).astype(jnp.float32)
        query_part = columns(query)
        key_part = columns(key_in)
        value_part = columns(value)
        cotan_part = columns(cotangent)
        rates = lax.dynamic_index_in_dim(decay_rate, head_index, 0, keepdims=False)
        coeffs = lax.dynamic_index_in_dim(coefficient, head_index, 0, keepdims=False)
        norms = lax.dynamic_index_in_dim(norm_factor, head_index, 0, keepdims=False)
        powers = jnp.exp(-rates[:, None] * positions[None, :])
        kernel = jnp.dot(coeffs, powers, precision=lax.Precision.HIGHEST)
        kernel_spec = jnp.fft.rfft(kernel, n=fft_length)
        product = key_part * value_part
        product_spec = jnp.fft.rfft(product, n=fft_length, axis=0)
        convolved = jnp.fft.irfft(product_spec * kernel_spec[:, None], n=fft_length, axis=0)[:LEN]
        mixed = (query_part * convolved).astype(jnp.bfloat16)
        grad_conv = cotan_part * query_part
        grad_query = (cotan_part * convolved).astype(jnp.bfloat16)
        grad_spec = jnp.fft.rfft(grad_conv[::-1], n=fft_length, axis=0)
        grad_product = jnp.fft.irfft(grad_spec * kernel_spec[:, None], n=fft_length, axis=0)[:LEN][::-1]
        grad_key = (grad_product * value_part).astype(jnp.bfloat16)
        grad_value = (grad_product * key_part).astype(jnp.bfloat16)
        lag_sums = jnp.fft.irfft(lax.optimization_barrier(jnp.sum(product_spec * grad_spec, axis=1)), n=fft_length)[:LEN][::-1]
        head_grad = norms * jnp.dot(powers, lag_sums, precision=lax.Precision.HIGHEST)
        return (mixed, grad_query, grad_key, grad_value, head_grad)
    outputs = lax.map(head_terms, jnp.arange(HEADS, dtype=jnp.int32))

    def to_rows(stacked):
        return jnp.transpose(stacked, (1, 0, 2)).reshape(LEN, HEADS * HEAD_DIM)
    residue_grad = outputs[4] / math.sqrt(float(LEN * HEAD_DIM))
    return (to_rows(outputs[0]), to_rows(outputs[1]), to_rows(outputs[2]), to_rows(outputs[3]), residue_grad)
```

```python
import functools
import math

import jax
import jax.numpy as jnp
from jax import lax
from jax.experimental import pallas as pl
from jax.experimental.pallas import tpu as pltpu
from jax.sharding import PartitionSpec as P

F32 = jnp.float32
BF16 = jnp.bfloat16
LAST = (((1,), (1,)), ((), ()))


def split(x):
    high = x.astype(BF16)
    return high, (x - high.astype(F32)).astype(BF16)


def mm(a, b):
    return jnp.dot(a, b, preferred_element_type=F32)


def mm_t(a, b):
    return lax.dot_general(a, b, LAST, preferred_element_type=F32)


def lanes(a, b):
    return jnp.concatenate([a, b], axis=1)


def state_kernel(group, width, poles, q_ref, k_ref, v_ref, c_ref, pc_ref, pr_ref, s_ref, near_ref):
    rows = q_ref.shape[0]
    place_l = lax.broadcasted_iota(jnp.int32, (poles, rows), 1).astype(F32)
    place_s = lax.broadcasted_iota(jnp.int32, (rows, poles), 0).astype(F32)
    lower = lax.broadcasted_iota(jnp.int32, (rows, rows), 0) >= lax.broadcasted_iota(
        jnp.int32, (rows, rows), 1
    )
    for h in range(group):
        cols = slice(h * width, (h + 1) * width)
        rate = pc_ref[h, :, 0:1]
        rate_row = pr_ref[h, 0:1, :poles]
        ph, pl_ = split(k_ref[:, cols].astype(F32) * v_ref[:, cols].astype(F32))
        gh, gl = split(c_ref[:, cols].astype(F32) * q_ref[:, cols].astype(F32))
        for d, (hi, lo, lag) in enumerate(
            ((ph, pl_, rows - 1.0 - place_l), (gh, gl, place_l))
        ):
            wide = mm(jnp.concatenate(split(jnp.exp(-rate * lag)), axis=0), lanes(hi, lo))
            s_ref[0, d, h] = (wide[:poles, :width] + wide[:poles, width:]) + (
                wide[poles:, :width] + wide[poles:, width:]
            )
        cross = mm_t(lanes(gh, gl), lanes(ph, ph)) + mm_t(gh, pl_)
        xh, xl = split(jnp.where(lower, cross, 0.0))
        wh, wl = split(jnp.exp(rate * place_l))
        grown = mm_t(xh, jnp.concatenate([wh, wl], axis=0))
        grown = grown[:, :poles] + grown[:, poles:] + mm_t(xl, wh)
        near_ref[h] = jnp.sum(grown * jnp.exp(-rate_row * place_s), axis=0, keepdims=True)


def chain_kernel(
    near_group, s_ref, near_ref, lam_ref, scale_ref, ent_ref, res_ref,
    pair, npair, chip, plane, tot, zed, back, got, stage, farb, resb,
    pair_s, pair_r, plane_s, plane_r, zed_s, zed_r, back_s, back_r, ent_s, ent_r, res_s, res_r,
):
    core = lax.axis_index("head")
    ctx = lax.axis_index("ctx")
    n_ctx = lax.axis_size("ctx")
    other = 1 - core
    q_n = near_group
    z_n = n_ctx // q_n
    z = ctx // q_n
    q = ctx % q_n

    def remote(src, dst, ss, rs, where):
        return pltpu.make_async_remote_copy(
            src_ref=src, dst_ref=dst, send_sem=ss, recv_sem=rs,
            device_id=where, device_id_type=pl.DeviceIdType.MESH,
        )

    barrier = pltpu.get_barrier_semaphore()
    pl.semaphore_signal(
        barrier, inc=1, device_id=(ctx, other), device_id_type=pl.DeviceIdType.MESH
    )
    for k in range(1, n_ctx):
        pl.semaphore_signal(
            barrier, inc=1, device_id=((ctx + k) % n_ctx, core),
            device_id_type=pl.DeviceIdType.MESH,
        )
    pl.semaphore_wait(barrier, n_ctx)

    first = [
        remote(s_ref.at[other], pair.at[core], pair_s.at[0], pair_r.at[0], (ctx, other)),
        remote(near_ref.at[other], npair.at[core], pair_s.at[1], pair_r.at[1], (ctx, other)),
    ]
    for copy in first:
        copy.start()
    pair[core] = s_ref[core]
    npair[core] = near_ref[core]
    for copy in first:
        copy.wait()

    plane_copies = []
    for k in range(1, q_n + 1):
        to = (q + k) % q_n
        lam = lam_ref[0, core, to]
        chip[to, 0] = lam * pair[0, 0, to] + pair[1, 0, to]
        chip[to, 1] = pair[0, 1, to] + lam * pair[1, 1, to]
        if k < q_n:
            copy = remote(
                chip.at[to], plane.at[q], plane_s.at[to], plane_r.at[q], (z * q_n + to, core)
            )
            copy.start()
            plane_copies.append(copy)
    plane[q] = chip[q]
    for k in range(1, q_n):
        src = (q + k) % q_n
        remote(
            chip.at[src], plane.at[src], plane_s.at[src], plane_r.at[src], (z * q_n + src, core)
        ).wait_recv()
    lam2 = lam_ref[1, core, q]
    fwd = plane[0, 0]
    bwd = plane[q_n - 1, 1]
    for j in range(1, q_n):
        fwd = lam2 * fwd + plane[j, 0]
        bwd = lam2 * bwd + plane[q_n - 1 - j, 1]
    tot[0] = fwd
    tot[1] = bwd
    zed_copies = []
    for k in range(1, z_n):
        to = (z + k) % z_n
        way = (to < z).astype(jnp.int32)
        copy = remote(
            tot.at[way], zed.at[z], zed_s.at[to], zed_r.at[z], (to * q_n + q, core)
        )
        copy.start()
        zed_copies.append(copy)
    zed[z] = jnp.zeros_like(fwd)
    for k in range(1, z_n):
        src = (z + k) % z_n
        remote(
            tot.at[0], zed.at[src], zed_s.at[src], zed_r.at[src], (src * q_n + q, core)
        ).wait_recv()
    lam3 = lam_ref[2, core, q]
    fwd = jnp.zeros_like(fwd)
    bwd = jnp.zeros_like(bwd)
    for j in range(z_n):
        use = (j < z).astype(F32)
        fwd = fwd + use * ((lam3 - 1.0) * fwd + zed[j])
        late = z_n - 1 - j
        use = (late > z).astype(F32)
        bwd = bwd + use * ((lam3 - 1.0) * bwd + zed[late])
    for j in range(q_n):
        back[j, 0] = fwd
        back[q_n - 1 - j, 1] = bwd
        fwd = lam2 * fwd + plane[j, 0]
        bwd = lam2 * bwd + plane[q_n - 1 - j, 1]
    back_copies = []
    for k in range(1, q_n):
        to = (q + k) % q_n
        copy = remote(back.at[to], got.at[q], back_s.at[to], back_r.at[q], (z * q_n + to, core))
        copy.start()
        back_copies.append(copy)
    got[q] = back[q]
    for k in range(1, q_n):
        src = (q + k) % q_n
        remote(
            back.at[src], got.at[src], back_s.at[src], back_r.at[src], (z * q_n + src, core)
        ).wait_recv()

    for j in range(q_n):
        lam = lam_ref[0, core, j]
        fwd = got[j, 0]
        bwd = got[j, 1]
        stage[0, 0, j] = fwd
        after = lam * fwd + pair[0, 0, j]
        stage[1, 0, j] = after
        stage[1, 1, j] = bwd
        stage[0, 1, j] = lam * bwd + pair[1, 1, j]
        farb[j] = pair[0, 1, j] * fwd + pair[1, 1, j] * after
    last = remote(stage.at[other], ent_ref.at[core], ent_s, ent_r, (ctx, other))
    last.start()
    ent_ref[core] = stage[core]

    owned, poles, width = farb.shape[1:]
    far = farb[...].reshape(q_n * owned * poles, width).T
    far = jnp.sum(far, axis=0, keepdims=True)
    resb[ctx] = npair[0] + npair[1] + scale_ref[0, core] * far
    res_copies = []
    for k in range(1, n_ctx):
        to = (ctx + k) % n_ctx
        copy = remote(resb.at[ctx], resb.at[ctx], res_s.at[to], res_r.at[ctx], (to, core))
        copy.start()
        res_copies.append(copy)
    for k in range(1, n_ctx):
        src = (ctx + k) % n_ctx
        remote(resb.at[src], resb.at[src], res_s.at[src], res_r.at[src], (src, core)).wait_recv()
    total = resb[0]
    for j in range(1, n_ctx):
        total = total + resb[j]
    res_ref[...] = scale_ref[1, core] * total
    last.wait()
    for copy in plane_copies + zed_copies + back_copies + res_copies:
        copy.wait_send()


def conv_kernel(
    group, width, poles, q_ref, k_ref, v_ref, c_ref, pc_ref, pr_ref, e_ref,
    mixed_ref, gq_ref, gk_ref, gv_ref,
):
    rows = q_ref.shape[0]
    place_l = lax.broadcasted_iota(jnp.int32, (poles, rows), 1).astype(F32)
    place_s = lax.broadcasted_iota(jnp.int32, (rows, 3 * poles), 0).astype(F32)
    lane = lax.broadcasted_iota(jnp.int32, (rows, 3 * poles), 1)
    middle = (lane >= poles) & (lane < 2 * poles)
    row_id = lax.broadcasted_iota(jnp.int32, (rows, rows), 0)
    col_id = lax.broadcasted_iota(jnp.int32, (rows, rows), 1)

    def left(x):
        high = x.astype(BF16).astype(F32)
        return jnp.where(middle, x - high, high).astype(BF16)

    def right(x):
        high, low = split(x)
        return jnp.concatenate([high, high, low], axis=0)

    def convolve(a, table, state, keep, hi, lo):
        wide = mm(a, lanes(right(state), right(table)))
        th, tl = split(jnp.where(keep, wide[:, width:], 0.0))
        inner = mm(th, lanes(hi, lo))
        return (inner[:, :width] + wide[:, :width]) + (inner[:, width:] + mm(tl, hi))

    for h in range(group):
        cols = slice(h * width, (h + 1) * width)
        rate = pc_ref[h, :, 0:1]
        coef = pc_ref[h, :, 1:2]
        step = pc_ref[h, :, 2:3]
        late = pc_ref[h, :, 3:4]
        rate_row = pr_ref[h, 0:1]
        coef_row = pr_ref[h, 1:2]
        query = q_ref[:, cols].astype(F32)
        key = k_ref[:, cols].astype(F32)
        value = v_ref[:, cols].astype(F32)
        cotan = c_ref[:, cols].astype(F32)
        ph, pl_ = split(key * value)
        gh, gl = split(cotan * query)
        decay_l = jnp.exp(-rate * place_l)
        growth_l = jnp.exp(rate * place_l)
        conv = convolve(
            left(coef_row * jnp.exp(-rate_row * place_s)),
            growth_l, step * e_ref[0, 0, h], row_id >= col_id, ph, pl_,
        )
        mixed_ref[:, cols] = (query * conv).astype(BF16)
        gq_ref[:, cols] = (cotan * conv).astype(BF16)
        gprod = convolve(
            left(jnp.exp(rate_row * place_s)),
            coef * decay_l, late * e_ref[0, 1, h], row_id <= col_id, gh, gl,
        )
        gk_ref[:, cols] = (gprod * value).astype(BF16)
        gv_ref[:, cols] = (gprod * key).astype(BF16)


def on_device(query, key_in, value, cotangent, decay_rate, residue):
    rows, features = query.shape
    heads, poles = decay_rate.shape
    width = features // heads
    n_ctx, cores = lax.axis_size("ctx"), lax.axis_size("head")
    half = heads // cores
    near_group = max(g for g in (1, 2, 4) if n_ctx % g == 0 and half % g == 0)
    owned = half // near_group
    group = max(g for g in (1, 2, 3, 4) if half % g == 0)
    per_half = half // group
    steps = heads // group

    norm = jnp.sqrt(-jnp.expm1(-2.0 * decay_rate))
    coef = residue * norm
    one = jnp.exp(-decay_rate)
    late = coef * jnp.exp(-decay_rate * rows)
    pc = jnp.stack([decay_rate, coef, one, late], axis=-1)
    pr = jnp.tile(jnp.stack([decay_rate, coef], axis=1), (1, 1, 3))
    spans = jnp.array([1.0, cores, cores * near_group], F32) * rows
    lam = jnp.exp(-spans[:, None, None] * decay_rate[None])
    lam = lam.reshape(3, cores, near_group, owned, poles, 1)
    total_rows = rows * n_ctx * cores
    scale = jnp.stack([one, norm / math.sqrt(float(total_rows * width))])
    scale = scale.reshape(2, cores, 1, half * poles)

    big = pl.BlockSpec((rows, group * width), lambda g: (0, g))
    pc_spec = pl.BlockSpec((group, poles, 4), lambda g: (g, 0, 0))
    pr_spec = pl.BlockSpec((group, 2, 3 * poles), lambda g: (g, 0, 0))
    state_spec = pl.BlockSpec(
        (1, 2, group, poles, width), lambda g: (g // per_half, 0, g % per_half, 0, 0)
    )
    state_shape = jax.ShapeDtypeStruct((cores, 2, half, poles, width), F32)
    limit = 32 * 2**20
    flops = 2 * heads * rows * rows * width
    area = rows * features * 2

    states, near = pl.pallas_call(
        functools.partial(state_kernel, group, width, poles),
        grid=(steps,),
        in_specs=[big] * 4 + [pc_spec, pr_spec],
        out_specs=[state_spec, pl.BlockSpec((group, 1, poles), lambda g: (g, 0, 0))],
        out_shape=[state_shape, jax.ShapeDtypeStruct((heads, 1, poles), F32)],
        compiler_params=pltpu.CompilerParams(vmem_limit_bytes=limit),
        cost_estimate=pl.CostEstimate(
            flops=5 * flops, bytes_accessed=4 * area, transcendentals=0
        ),
        name="states",
    )(query, key_in, value, cotangent, pc, pr)

    in_vmem = pl.BlockSpec(memory_space=pltpu.VMEM)
    part = (owned, poles, width)
    sem = pltpu.SemaphoreType.DMA
    z_n = n_ctx // near_group
    entering, res = pl.pallas_call(
        functools.partial(chain_kernel, near_group),
        in_specs=[in_vmem] * 4,
        out_specs=[in_vmem] * 2,
        out_shape=[
            jax.ShapeDtypeStruct((cores, 2, near_group) + part, F32),
            jax.ShapeDtypeStruct((1, half * poles), F32),
        ],
        scratch_shapes=[
            pltpu.VMEM((cores, 2, near_group) + part, F32),
            pltpu.VMEM((cores, 1, half * poles), F32),
            pltpu.VMEM((near_group, 2) + part, F32),
            pltpu.VMEM((near_group, 2) + part, F32),
            pltpu.VMEM((2,) + part, F32),
            pltpu.VMEM((z_n,) + part, F32),
            pltpu.VMEM((near_group, 2) + part, F32),
            pltpu.VMEM((near_group, 2) + part, F32),
            pltpu.VMEM((cores, 2, near_group) + part, F32),
            pltpu.VMEM((near_group,) + part, F32),
            pltpu.VMEM((n_ctx, 1, half * poles), F32),
            sem((2,)), sem((2,)),
            sem((near_group,)), sem((near_group,)),
            sem((z_n,)), sem((z_n,)),
            sem((near_group,)), sem((near_group,)),
            sem, sem,
            sem((n_ctx,)), sem((n_ctx,)),
        ],
        compiler_params=pltpu.CompilerParams(
            collective_id=0, has_side_effects=True, vmem_limit_bytes=limit
        ),
        name="chain",
    )(
        states.reshape((cores, 2, near_group) + part),
        near.reshape(cores, 1, half * poles), lam, scale,
    )

    outs = pl.pallas_call(
        functools.partial(conv_kernel, group, width, poles),
        grid=(steps,),
        in_specs=[big] * 4 + [pc_spec, pr_spec, state_spec],
        out_specs=[big] * 4,
        out_shape=[jax.ShapeDtypeStruct((rows, features), BF16)] * 4,
        compiler_params=pltpu.CompilerParams(vmem_limit_bytes=limit),
        cost_estimate=pl.CostEstimate(
            flops=8 * flops, bytes_accessed=8 * area, transcendentals=0
        ),
        name="convolve",
    )(
        query, key_in, value, cotangent, pc, pr,
        entering.reshape(cores, 2, half, poles, width),
    )
    return (*outs, res.reshape(half, poles))


def solution(mesh):
    wide = P(("ctx", "head"), None)
    return jax.shard_map(
        on_device,
        mesh=mesh,
        in_specs=(wide, wide, wide, wide, P(), P()),
        out_specs=(wide, wide, wide, wide, P("head", None)),
        check_vma=False,
    )
```

```python
import functools
import math

import jax
import jax.numpy as jnp
from jax import lax
from jax.experimental import pallas as pl
from jax.experimental.pallas import tpu as pltpu
from jax.sharding import PartitionSpec as P

F32 = jnp.float32
BF16 = jnp.bfloat16
LAST = (((1,), (1,)), ((), ()))


def split(x):
    high = x.astype(BF16)
    return high, (x - high.astype(F32)).astype(BF16)


def mm(a, b):
    return jnp.dot(a, b, preferred_element_type=F32)


def mm_t(a, b):
    return lax.dot_general(a, b, LAST, preferred_element_type=F32)


def column(row):
    count = row.shape[1]
    same = lax.broadcasted_iota(jnp.int32, (count, count), 0) == lax.broadcasted_iota(
        jnp.int32, (count, count), 1
    )
    return jnp.sum(jnp.where(same, row, 0.0), axis=1, keepdims=True)


def lanes(a, b):
    return jnp.concatenate([a, b], axis=1)


def state_kernel(
    group, width, poles, share, q_ref, k_ref, v_ref, c_ref, rate_ref, norm_ref,
    s_ref, near_ref, par_ref,
):
    rows = q_ref.shape[0]
    place_l = lax.broadcasted_iota(jnp.int32, (poles, rows), 1).astype(F32)
    place_s = lax.broadcasted_iota(jnp.int32, (rows, poles), 0).astype(F32)
    lower = lax.broadcasted_iota(jnp.int32, (rows, rows), 0) >= lax.broadcasted_iota(
        jnp.int32, (rows, rows), 1
    )
    for h in range(group):
        cols = slice(h * width, (h + 1) * width)
        rate_row = rate_ref[h : h + 1, :]
        norm_row = norm_ref[h : h + 1, :] * share
        rate = column(rate_row)
        far_scale = column(norm_row * jnp.exp(-rate_row))
        lane = lax.broadcasted_iota(jnp.int32, (poles, width), 1)
        par_ref[0, h] = jnp.where(lane == 0, rate, far_scale)
        ph, pl_ = split(k_ref[:, cols].astype(F32) * v_ref[:, cols].astype(F32))
        gh, gl = split(c_ref[:, cols].astype(F32) * q_ref[:, cols].astype(F32))
        for d, (hi, lo, lag) in enumerate(
            ((ph, pl_, rows - 1.0 - place_l), (gh, gl, place_l))
        ):
            wide = mm(jnp.concatenate(split(jnp.exp(-rate * lag)), axis=0), lanes(hi, lo))
            s_ref[0, d, h] = (wide[:poles, :width] + wide[:poles, width:]) + (
                wide[poles:, :width] + wide[poles:, width:]
            )
        cross = mm_t(lanes(gh, gl), lanes(ph, ph)) + mm_t(gh, pl_)
        xh, xl = split(jnp.where(lower, cross, 0.0))
        wh, wl = split(jnp.exp(rate * place_l))
        grown = mm_t(xh, jnp.concatenate([wh, wl], axis=0))
        grown = grown[:, :poles] + grown[:, poles:] + mm_t(xl, wh)
        near = jnp.sum(grown * jnp.exp(-rate_row * place_s), axis=0, keepdims=True)
        near_ref[h : h + 1, :] = norm_row * near


def chain_kernel(
    near_group, rows, s_ref, near_ref, par_ref, ent_ref, res_ref,
    pair, npair, chip, plane, tot, zed, back, got, stage, farb, resb,
    pair_s, pair_r, plane_s, plane_r, zed_s, zed_r, back_s, back_r, ent_s, ent_r, res_s, res_r,
):
    core = lax.axis_index("head")
    ctx = lax.axis_index("ctx")
    n_ctx = lax.axis_size("ctx")
    other = 1 - core
    q_n = near_group
    z_n = n_ctx // q_n
    z = ctx // q_n
    q = ctx % q_n

    def remote(src, dst, ss, rs, where):
        return pltpu.make_async_remote_copy(
            src_ref=src, dst_ref=dst, send_sem=ss, recv_sem=rs,
            device_id=where, device_id_type=pl.DeviceIdType.MESH,
        )

    def decay(slot, count):
        return jnp.exp(par_ref[core, slot, :, :, 0:1] * (-float(rows * count)))

    barrier = pltpu.get_barrier_semaphore()
    pl.semaphore_signal(
        barrier, inc=1, device_id=(ctx, other), device_id_type=pl.DeviceIdType.MESH
    )
    for k in range(1, n_ctx):
        pl.semaphore_signal(
            barrier, inc=1, device_id=((ctx + k) % n_ctx, core),
            device_id_type=pl.DeviceIdType.MESH,
        )
    pl.semaphore_wait(barrier, n_ctx)

    first = [
        remote(s_ref.at[other], pair.at[core], pair_s.at[0], pair_r.at[0], (ctx, other)),
        remote(near_ref.at[other], npair.at[core], pair_s.at[1], pair_r.at[1], (ctx, other)),
    ]
    for copy in first:
        copy.start()
    pair[core] = s_ref[core]
    npair[core] = near_ref[core]
    for copy in first:
        copy.wait()

    plane_copies = []
    for k in range(1, q_n + 1):
        to = (q + k) % q_n
        lam = decay(to, 1)
        chip[to, 0] = lam * pair[0, 0, to] + pair[1, 0, to]
        chip[to, 1] = pair[0, 1, to] + lam * pair[1, 1, to]
        if k < q_n:
            copy = remote(
                chip.at[to], plane.at[q], plane_s.at[to], plane_r.at[q], (z * q_n + to, core)
            )
            copy.start()
            plane_copies.append(copy)
    plane[q] = chip[q]
    for k in range(1, q_n):
        src = (q + k) % q_n
        remote(
            chip.at[src], plane.at[src], plane_s.at[src], plane_r.at[src], (z * q_n + src, core)
        ).wait_recv()
    lam2 = decay(q, 2)
    fwd = plane[0, 0]
    bwd = plane[q_n - 1, 1]
    for j in range(1, q_n):
        fwd = lam2 * fwd + plane[j, 0]
        bwd = lam2 * bwd + plane[q_n - 1 - j, 1]
    tot[0] = fwd
    tot[1] = bwd
    zed_copies = []
    for k in range(1, z_n):
        to = (z + k) % z_n
        way = (to < z).astype(jnp.int32)
        copy = remote(
            tot.at[way], zed.at[z], zed_s.at[to], zed_r.at[z], (to * q_n + q, core)
        )
        copy.start()
        zed_copies.append(copy)
    zed[z] = jnp.zeros_like(fwd)
    for k in range(1, z_n):
        src = (z + k) % z_n
        remote(
            tot.at[0], zed.at[src], zed_s.at[src], zed_r.at[src], (src * q_n + q, core)
        ).wait_recv()
    lam3 = decay(q, 2 * q_n)
    fwd = jnp.zeros_like(fwd)
    bwd = jnp.zeros_like(bwd)
    for j in range(z_n):
        use = (j < z).astype(F32)
        fwd = fwd + use * ((lam3 - 1.0) * fwd + zed[j])
        late = z_n - 1 - j
        use = (late > z).astype(F32)
        bwd = bwd + use * ((lam3 - 1.0) * bwd + zed[late])
    for j in range(q_n):
        back[j, 0] = fwd
        back[q_n - 1 - j, 1] = bwd
        fwd = lam2 * fwd + plane[j, 0]
        bwd = lam2 * bwd + plane[q_n - 1 - j, 1]
    back_copies = []
    for k in range(1, q_n):
        to = (q + k) % q_n
        copy = remote(back.at[to], got.at[q], back_s.at[to], back_r.at[q], (z * q_n + to, core))
        copy.start()
        back_copies.append(copy)
    got[q] = back[q]
    for k in range(1, q_n):
        src = (q + k) % q_n
        remote(
            back.at[src], got.at[src], back_s.at[src], back_r.at[src], (z * q_n + src, core)
        ).wait_recv()

    for j in range(q_n):
        lam = decay(j, 1)
        fwd = got[j, 0]
        bwd = got[j, 1]
        stage[0, 0, j] = fwd
        after = lam * fwd + pair[0, 0, j]
        stage[1, 0, j] = after
        stage[1, 1, j] = bwd
        stage[0, 1, j] = lam * bwd + pair[1, 1, j]
        farb[j] = par_ref[core, j, :, :, 1:2] * (pair[0, 1, j] * fwd + pair[1, 1, j] * after)
    last = remote(stage.at[other], ent_ref.at[core], ent_s, ent_r, (ctx, other))
    last.start()
    ent_ref[core] = stage[core]

    owned, poles, width = farb.shape[1:]
    far = jnp.sum(farb[...].reshape(q_n * owned, poles, width), axis=-1)
    resb[ctx] = npair[0] + npair[1] + far
    res_copies = []
    for k in range(1, n_ctx):
        to = (ctx + k) % n_ctx
        copy = remote(resb.at[ctx], resb.at[ctx], res_s.at[to], res_r.at[ctx], (to, core))
        copy.start()
        res_copies.append(copy)
    for k in range(1, n_ctx):
        src = (ctx + k) % n_ctx
        remote(resb.at[src], resb.at[src], res_s.at[src], res_r.at[src], (src, core)).wait_recv()
    total = resb[0]
    for j in range(1, n_ctx):
        total = total + resb[j]
    res_ref[...] = total
    last.wait()
    for copy in plane_copies + zed_copies + back_copies + res_copies:
        copy.wait_send()


def conv_kernel(
    group, width, poles, q_ref, k_ref, v_ref, c_ref, rate_ref, norm_ref, residue_ref, e_ref,
    mixed_ref, gq_ref, gk_ref, gv_ref,
):
    rows = q_ref.shape[0]
    place_l = lax.broadcasted_iota(jnp.int32, (poles, rows), 1).astype(F32)
    place_s = lax.broadcasted_iota(jnp.int32, (rows, 3 * poles), 0).astype(F32)
    lane = lax.broadcasted_iota(jnp.int32, (rows, 3 * poles), 1)
    middle = (lane >= poles) & (lane < 2 * poles)
    tiled = lax.broadcasted_iota(jnp.int32, (poles, 3 * poles), 0) == lax.rem(
        lax.broadcasted_iota(jnp.int32, (poles, 3 * poles), 1), poles
    )
    row_id = lax.broadcasted_iota(jnp.int32, (rows, rows), 0)
    col_id = lax.broadcasted_iota(jnp.int32, (rows, rows), 1)

    def left(x):
        high = x.astype(BF16).astype(F32)
        return jnp.where(middle, x - high, high).astype(BF16)

    def right(x):
        high, low = split(x)
        return jnp.concatenate([high, high, low], axis=0)

    def convolve(a, table, state, keep, hi, lo):
        wide = mm(a, lanes(right(state), right(table)))
        th, tl = split(jnp.where(keep, wide[:, width:], 0.0))
        inner = mm(th, lanes(hi, lo))
        return (inner[:, :width] + wide[:, :width]) + (inner[:, width:] + mm(tl, hi))

    for h in range(group):
        cols = slice(h * width, (h + 1) * width)
        rate = column(rate_ref[h : h + 1, :])
        coef = column(norm_ref[h : h + 1, :] * residue_ref[h : h + 1, :])
        step = jnp.exp(-rate)
        late = coef * jnp.exp(rate * (-float(rows)))
        rate_row = jnp.sum(jnp.where(tiled, rate, 0.0), axis=0, keepdims=True)
        coef_row = jnp.sum(jnp.where(tiled, coef, 0.0), axis=0, keepdims=True)
        query = q_ref[:, cols].astype(F32)
        key = k_ref[:, cols].astype(F32)
        value = v_ref[:, cols].astype(F32)
        cotan = c_ref[:, cols].astype(F32)
        ph, pl_ = split(key * value)
        gh, gl = split(cotan * query)
        decay_l = jnp.exp(-rate * place_l)
        growth_l = jnp.exp(rate * place_l)
        conv = convolve(
            left(coef_row * jnp.exp(-rate_row * place_s)),
            growth_l, step * e_ref[0, 0, h], row_id >= col_id, ph, pl_,
        )
        mixed_ref[:, cols] = (query * conv).astype(BF16)
        gq_ref[:, cols] = (cotan * conv).astype(BF16)
        gprod = convolve(
            left(jnp.exp(rate_row * place_s)),
            coef * decay_l, late * e_ref[0, 1, h], row_id <= col_id, gh, gl,
        )
        gk_ref[:, cols] = (gprod * value).astype(BF16)
        gv_ref[:, cols] = (gprod * key).astype(BF16)


def on_device(query, key_in, value, cotangent, decay_rate, residue):
    rows, features = query.shape
    heads, poles = decay_rate.shape
    width = features // heads
    n_ctx, cores = lax.axis_size("ctx"), lax.axis_size("head")
    half = heads // cores
    near_group = max(g for g in (1, 2, 4) if n_ctx % g == 0 and half % g == 0)
    owned = half // near_group
    group = 8 if half % 8 == 0 else half
    per_half = half // group
    steps = heads // group

    norm = jnp.sqrt(-jnp.expm1(-2.0 * decay_rate))
    share = 1.0 / math.sqrt(float(rows * n_ctx * cores * width))

    big = pl.BlockSpec((rows, group * width), lambda g: (0, g))
    par_spec = pl.BlockSpec((group, poles), lambda g: (g, 0))
    state_spec = pl.BlockSpec(
        (1, 2, group, poles, width), lambda g: (g // per_half, 0, g % per_half, 0, 0)
    )
    state_shape = jax.ShapeDtypeStruct((cores, 2, half, poles, width), F32)
    limit = 60 * 2**20
    flops = 2 * heads * rows * rows * width
    area = rows * features * 2

    states, near, par = pl.pallas_call(
        functools.partial(state_kernel, group, width, poles, share),
        grid=(steps,),
        in_specs=[big] * 4 + [par_spec] * 2,
        out_specs=[
            state_spec,
            par_spec,
            pl.BlockSpec(
                (1, group, poles, width), lambda g: (g // per_half, g % per_half, 0, 0)
            ),
        ],
        out_shape=[
            state_shape,
            jax.ShapeDtypeStruct((heads, poles), F32),
            jax.ShapeDtypeStruct((cores, half, poles, width), F32),
        ],
        compiler_params=pltpu.CompilerParams(vmem_limit_bytes=limit),
        cost_estimate=pl.CostEstimate(
            flops=5 * flops, bytes_accessed=4 * area, transcendentals=0
        ),
        name="states",
    )(query, key_in, value, cotangent, decay_rate, norm)

    in_vmem = pl.BlockSpec(memory_space=pltpu.VMEM)
    part = (owned, poles, width)
    sem = pltpu.SemaphoreType.DMA
    z_n = n_ctx // near_group
    entering, res = pl.pallas_call(
        functools.partial(chain_kernel, near_group, rows),
        in_specs=[in_vmem] * 3,
        out_specs=[in_vmem] * 2,
        out_shape=[
            jax.ShapeDtypeStruct((cores, 2, near_group) + part, F32),
            jax.ShapeDtypeStruct((half, poles), F32),
        ],
        scratch_shapes=[
            pltpu.VMEM((cores, 2, near_group) + part, F32),
            pltpu.VMEM((cores, half, poles), F32),
            pltpu.VMEM((near_group, 2) + part, F32),
            pltpu.VMEM((near_group, 2) + part, F32),
            pltpu.VMEM((2,) + part, F32),
            pltpu.VMEM((z_n,) + part, F32),
            pltpu.VMEM((near_group, 2) + part, F32),
            pltpu.VMEM((near_group, 2) + part, F32),
            pltpu.VMEM((cores, 2, near_group) + part, F32),
            pltpu.VMEM((near_group,) + part, F32),
            pltpu.VMEM((n_ctx, half, poles), F32),
            sem((2,)), sem((2,)),
            sem((near_group,)), sem((near_group,)),
            sem((z_n,)), sem((z_n,)),
            sem((near_group,)), sem((near_group,)),
            sem, sem,
            sem((n_ctx,)), sem((n_ctx,)),
        ],
        compiler_params=pltpu.CompilerParams(
            collective_id=0, has_side_effects=True, vmem_limit_bytes=limit
        ),
        name="chain",
    )(
        states.reshape((cores, 2, near_group) + part),
        near.reshape(cores, half, poles), par.reshape((cores, near_group) + part),
    )

    outs = pl.pallas_call(
        functools.partial(conv_kernel, group, width, poles),
        grid=(steps,),
        in_specs=[big] * 4 + [par_spec] * 3 + [state_spec],
        out_specs=[big] * 4,
        out_shape=[jax.ShapeDtypeStruct((rows, features), BF16)] * 4,
        compiler_params=pltpu.CompilerParams(vmem_limit_bytes=limit),
        cost_estimate=pl.CostEstimate(
            flops=8 * flops, bytes_accessed=8 * area, transcendentals=0
        ),
        name="convolve",
    )(
        query, key_in, value, cotangent, decay_rate, norm, residue,
        entering.reshape(cores, 2, half, poles, width),
    )
    return (*outs, res)


def solution(mesh):
    wide = P(("ctx", "head"), None)
    return jax.shard_map(
        on_device,
        mesh=mesh,
        in_specs=(wide, wide, wide, wide, P(), P()),
        out_specs=(wide, wide, wide, wide, P("head", None)),
        check_vma=False,
    )
```

```python
import functools
import math

import jax
import jax.numpy as jnp
from jax import lax
from jax.experimental import pallas as pl
from jax.experimental.pallas import tpu as pltpu
from jax.sharding import PartitionSpec as P

F32 = jnp.float32
BF16 = jnp.bfloat16
LAST = (((1,), (1,)), ((), ()))


def split(x):
    high = x.astype(BF16)
    return high, (x - high.astype(F32)).astype(BF16)


def mm(a, b):
    return jnp.dot(a, b, preferred_element_type=F32)


def mm_t(a, b):
    return lax.dot_general(a, b, LAST, preferred_element_type=F32)


def pick(ref, place):
    lane = lax.broadcasted_iota(jnp.int32, ref.shape, 1)
    return jnp.sum(jnp.where(lane == place, ref[...], 0.0), axis=1, keepdims=True)


def as_row(column, repeats):
    count = column.shape[0]
    shape = (count, repeats * count)
    same = lax.broadcasted_iota(jnp.int32, shape, 0) == lax.rem(
        lax.broadcasted_iota(jnp.int32, shape, 1), count
    )
    return jnp.sum(jnp.where(same, column, 0.0), axis=0, keepdims=True)


def lanes(a, b):
    return jnp.concatenate([a, b], axis=1)


def state_kernel(
    group, width, poles, share, q_ref, k_ref, v_ref, c_ref, rate_ref, norm_ref,
    s_ref, near_ref, par_ref,
):
    rows = q_ref.shape[0]
    first = pl.program_id(0) * group
    place_l = lax.broadcasted_iota(jnp.int32, (poles, rows), 1).astype(F32)
    place_s = lax.broadcasted_iota(jnp.int32, (rows, poles), 0).astype(F32)
    lower = lax.broadcasted_iota(jnp.int32, (rows, rows), 0) >= lax.broadcasted_iota(
        jnp.int32, (rows, rows), 1
    )
    for h in range(group):
        cols = slice(h * width, (h + 1) * width)
        rate = pick(rate_ref, first + h)
        norm = pick(norm_ref, first + h) * share
        rate_row = as_row(rate, 1)
        norm_row = as_row(norm, 1)
        far_scale = norm * jnp.exp(-rate)
        lane = lax.broadcasted_iota(jnp.int32, (poles, width), 1)
        par_ref[0, h] = jnp.where(lane == 0, rate, far_scale)
        ph, pl_ = split(k_ref[:, cols].astype(F32) * v_ref[:, cols].astype(F32))
        gh, gl = split(c_ref[:, cols].astype(F32) * q_ref[:, cols].astype(F32))
        for d, (hi, lo, lag) in enumerate(
            ((ph, pl_, rows - 1.0 - place_l), (gh, gl, place_l))
        ):
            wide = mm(jnp.concatenate(split(jnp.exp(-rate * lag)), axis=0), lanes(hi, lo))
            s_ref[0, d, h] = (wide[:poles, :width] + wide[:poles, width:]) + (
                wide[poles:, :width] + wide[poles:, width:]
            )
        cross = mm_t(lanes(gh, gl), lanes(ph, ph)) + mm_t(gh, pl_)
        xh, xl = split(jnp.where(lower, cross, 0.0))
        wh, wl = split(jnp.exp(rate * place_l))
        grown = mm_t(xh, jnp.concatenate([wh, wl], axis=0))
        grown = grown[:, :poles] + grown[:, poles:] + mm_t(xl, wh)
        near = jnp.sum(grown * jnp.exp(-rate_row * place_s), axis=0, keepdims=True)
        near_ref[h : h + 1, :] = norm_row * near


def chain_kernel(
    near_group, rows, s_ref, near_ref, par_ref, ent_ref, res_ref,
    pair, npair, chip, plane, tot, zed, back, got, stage, farb, resb,
    pair_s, pair_r, plane_s, plane_r, zed_s, zed_r, back_s, back_r, ent_s, ent_r, res_s, res_r,
):
    core = lax.axis_index("head")
    ctx = lax.axis_index("ctx")
    n_ctx = lax.axis_size("ctx")
    other = 1 - core
    q_n = near_group
    z_n = n_ctx // q_n
    z = ctx // q_n
    q = ctx % q_n

    def remote(src, dst, ss, rs, where):
        return pltpu.make_async_remote_copy(
            src_ref=src, dst_ref=dst, send_sem=ss, recv_sem=rs,
            device_id=where, device_id_type=pl.DeviceIdType.MESH,
        )

    def decay(slot, count):
        return jnp.exp(par_ref[core, slot, :, :, 0:1] * (-float(rows * count)))

    barrier = pltpu.get_barrier_semaphore()
    pl.semaphore_signal(
        barrier, inc=1, device_id=(ctx, other), device_id_type=pl.DeviceIdType.MESH
    )
    for k in range(1, n_ctx):
        pl.semaphore_signal(
            barrier, inc=1, device_id=((ctx + k) % n_ctx, core),
            device_id_type=pl.DeviceIdType.MESH,
        )
    pl.semaphore_wait(barrier, n_ctx)

    first = [
        remote(s_ref.at[other], pair.at[core], pair_s.at[0], pair_r.at[0], (ctx, other)),
        remote(near_ref.at[other], npair.at[core], pair_s.at[1], pair_r.at[1], (ctx, other)),
    ]
    for copy in first:
        copy.start()
    pair[core] = s_ref[core]
    npair[core] = near_ref[core]
    for copy in first:
        copy.wait()

    plane_copies = []
    for k in range(1, q_n + 1):
        to = (q + k) % q_n
        lam = decay(to, 1)
        chip[to, 0] = lam * pair[0, 0, to] + pair[1, 0, to]
        chip[to, 1] = pair[0, 1, to] + lam * pair[1, 1, to]
        if k < q_n:
            copy = remote(
                chip.at[to], plane.at[q], plane_s.at[to], plane_r.at[q], (z * q_n + to, core)
            )
            copy.start()
            plane_copies.append(copy)
    plane[q] = chip[q]
    for k in range(1, q_n):
        src = (q + k) % q_n
        remote(
            chip.at[src], plane.at[src], plane_s.at[src], plane_r.at[src], (z * q_n + src, core)
        ).wait_recv()
    lam2 = decay(q, 2)
    fwd = plane[0, 0]
    bwd = plane[q_n - 1, 1]
    for j in range(1, q_n):
        fwd = lam2 * fwd + plane[j, 0]
        bwd = lam2 * bwd + plane[q_n - 1 - j, 1]
    tot[0] = fwd
    tot[1] = bwd
    zed_copies = []
    for k in range(1, z_n):
        to = (z + k) % z_n
        way = (to < z).astype(jnp.int32)
        copy = remote(
            tot.at[way], zed.at[z], zed_s.at[to], zed_r.at[z], (to * q_n + q, core)
        )
        copy.start()
        zed_copies.append(copy)
    zed[z] = jnp.zeros_like(fwd)
    for k in range(1, z_n):
        src = (z + k) % z_n
        remote(
            tot.at[0], zed.at[src], zed_s.at[src], zed_r.at[src], (src * q_n + q, core)
        ).wait_recv()
    lam3 = decay(q, 2 * q_n)
    fwd = jnp.zeros_like(fwd)
    bwd = jnp.zeros_like(bwd)
    for j in range(z_n):
        use = (j < z).astype(F32)
        fwd = fwd + use * ((lam3 - 1.0) * fwd + zed[j])
        late = z_n - 1 - j
        use = (late > z).astype(F32)
        bwd = bwd + use * ((lam3 - 1.0) * bwd + zed[late])
    for j in range(q_n):
        back[j, 0] = fwd
        back[q_n - 1 - j, 1] = bwd
        fwd = lam2 * fwd + plane[j, 0]
        bwd = lam2 * bwd + plane[q_n - 1 - j, 1]
    back_copies = []
    for k in range(1, q_n):
        to = (q + k) % q_n
        copy = remote(back.at[to], got.at[q], back_s.at[to], back_r.at[q], (z * q_n + to, core))
        copy.start()
        back_copies.append(copy)
    got[q] = back[q]
    for k in range(1, q_n):
        src = (q + k) % q_n
        remote(
            back.at[src], got.at[src], back_s.at[src], back_r.at[src], (z * q_n + src, core)
        ).wait_recv()

    for j in range(q_n):
        lam = decay(j, 1)
        fwd = got[j, 0]
        bwd = got[j, 1]
        stage[0, 0, j] = fwd
        after = lam * fwd + pair[0, 0, j]
        stage[1, 0, j] = after
        stage[1, 1, j] = bwd
        stage[0, 1, j] = lam * bwd + pair[1, 1, j]
        farb[j] = par_ref[core, j, :, :, 1:2] * (pair[0, 1, j] * fwd + pair[1, 1, j] * after)
    last = remote(stage.at[other], ent_ref.at[core], ent_s, ent_r, (ctx, other))
    last.start()
    ent_ref[core] = stage[core]

    owned, poles, width = farb.shape[1:]
    far = jnp.sum(farb[...].reshape(q_n * owned, poles, width), axis=-1)
    resb[ctx] = npair[0] + npair[1] + far
    res_copies = []
    for k in range(1, n_ctx):
        to = (ctx + k) % n_ctx
        copy = remote(resb.at[ctx], resb.at[ctx], res_s.at[to], res_r.at[ctx], (to, core))
        copy.start()
        res_copies.append(copy)
    for k in range(1, n_ctx):
        src = (ctx + k) % n_ctx
        remote(resb.at[src], resb.at[src], res_s.at[src], res_r.at[src], (src, core)).wait_recv()
    total = resb[0]
    for j in range(1, n_ctx):
        total = total + resb[j]
    res_ref[...] = total.T
    last.wait()
    for copy in plane_copies + zed_copies + back_copies + res_copies:
        copy.wait_send()


def conv_kernel(
    group, width, poles, q_ref, k_ref, v_ref, c_ref, rate_ref, norm_ref, residue_ref, e_ref,
    mixed_ref, gq_ref, gk_ref, gv_ref,
):
    rows = q_ref.shape[0]
    first = pl.program_id(0) * group
    place_l = lax.broadcasted_iota(jnp.int32, (poles, rows), 1).astype(F32)
    place_s = lax.broadcasted_iota(jnp.int32, (rows, 3 * poles), 0).astype(F32)
    lane = lax.broadcasted_iota(jnp.int32, (rows, 3 * poles), 1)
    middle = (lane >= poles) & (lane < 2 * poles)
    row_id = lax.broadcasted_iota(jnp.int32, (rows, rows), 0)
    col_id = lax.broadcasted_iota(jnp.int32, (rows, rows), 1)

    def left(x):
        high = x.astype(BF16).astype(F32)
        return jnp.where(middle, x - high, high).astype(BF16)

    def right(x):
        high, low = split(x)
        return jnp.concatenate([high, high, low], axis=0)

    def convolve(a, table, state, keep, hi, lo):
        wide = mm(a, lanes(right(state), right(table)))
        th, tl = split(jnp.where(keep, wide[:, width:], 0.0))
        inner = mm(th, lanes(hi, lo))
        return (inner[:, :width] + wide[:, :width]) + (inner[:, width:] + mm(tl, hi))

    for h in range(group):
        cols = slice(h * width, (h + 1) * width)
        rate = pick(rate_ref, first + h)
        coef = pick(norm_ref, first + h) * pick(residue_ref, first + h)
        step = jnp.exp(-rate)
        late = coef * jnp.exp(rate * (-float(rows)))
        rate_row = as_row(rate, 3)
        coef_row = as_row(coef, 3)
        query = q_ref[:, cols].astype(F32)
        key = k_ref[:, cols].astype(F32)
        value = v_ref[:, cols].astype(F32)
        cotan = c_ref[:, cols].astype(F32)
        ph, pl_ = split(key * value)
        gh, gl = split(cotan * query)
        decay_l = jnp.exp(-rate * place_l)
        growth_l = jnp.exp(rate * place_l)
        conv = convolve(
            left(coef_row * jnp.exp(-rate_row * place_s)),
            growth_l, step * e_ref[0, 0, h], row_id >= col_id, ph, pl_,
        )
        mixed_ref[:, cols] = (query * conv).astype(BF16)
        gq_ref[:, cols] = (cotan * conv).astype(BF16)
        gprod = convolve(
            left(jnp.exp(rate_row * place_s)),
            coef * decay_l, late * e_ref[0, 1, h], row_id <= col_id, gh, gl,
        )
        gk_ref[:, cols] = (gprod * value).astype(BF16)
        gv_ref[:, cols] = (gprod * key).astype(BF16)


def on_device(query, key_in, value, cotangent, decay_rate, residue):
    rows, features = query.shape
    heads, poles = decay_rate.shape
    width = features // heads
    n_ctx, cores = lax.axis_size("ctx"), lax.axis_size("head")
    half = heads // cores
    near_group = max(g for g in (1, 2, 4) if n_ctx % g == 0 and half % g == 0)
    owned = half // near_group
    group = 8 if half % 8 == 0 else half
    per_half = half // group
    steps = heads // group

    rates, residues = decay_rate.T, residue.T
    norm = jnp.sqrt(-jnp.expm1(-2.0 * rates))
    share = 1.0 / math.sqrt(float(rows * n_ctx * cores * width))

    big = pl.BlockSpec((rows, group * width), lambda g: (0, g))
    par_spec = pl.BlockSpec((group, poles), lambda g: (g, 0))
    flat_spec = pl.BlockSpec((poles, heads), lambda g: (0, 0))
    state_spec = pl.BlockSpec(
        (1, 2, group, poles, width), lambda g: (g // per_half, 0, g % per_half, 0, 0)
    )
    state_shape = jax.ShapeDtypeStruct((cores, 2, half, poles, width), F32)
    limit = 60 * 2**20
    flops = 2 * heads * rows * rows * width
    area = rows * features * 2

    states, near, par = pl.pallas_call(
        functools.partial(state_kernel, group, width, poles, share),
        grid=(steps,),
        in_specs=[big] * 4 + [flat_spec] * 2,
        out_specs=[
            state_spec,
            par_spec,
            pl.BlockSpec(
                (1, group, poles, width), lambda g: (g // per_half, g % per_half, 0, 0)
            ),
        ],
        out_shape=[
            state_shape,
            jax.ShapeDtypeStruct((heads, poles), F32),
            jax.ShapeDtypeStruct((cores, half, poles, width), F32),
        ],
        compiler_params=pltpu.CompilerParams(vmem_limit_bytes=limit),
        cost_estimate=pl.CostEstimate(
            flops=5 * flops, bytes_accessed=4 * area, transcendentals=0
        ),
        name="states",
    )(query, key_in, value, cotangent, rates, norm)

    in_vmem = pl.BlockSpec(memory_space=pltpu.VMEM)
    part = (owned, poles, width)
    sem = pltpu.SemaphoreType.DMA
    z_n = n_ctx // near_group
    entering, res = pl.pallas_call(
        functools.partial(chain_kernel, near_group, rows),
        in_specs=[in_vmem] * 3,
        out_specs=[in_vmem] * 2,
        out_shape=[
            jax.ShapeDtypeStruct((cores, 2, near_group) + part, F32),
            jax.ShapeDtypeStruct((poles, half), F32),
        ],
        scratch_shapes=[
            pltpu.VMEM((cores, 2, near_group) + part, F32),
            pltpu.VMEM((cores, half, poles), F32),
            pltpu.VMEM((near_group, 2) + part, F32),
            pltpu.VMEM((near_group, 2) + part, F32),
            pltpu.VMEM((2,) + part, F32),
            pltpu.VMEM((z_n,) + part, F32),
            pltpu.VMEM((near_group, 2) + part, F32),
            pltpu.VMEM((near_group, 2) + part, F32),
            pltpu.VMEM((cores, 2, near_group) + part, F32),
            pltpu.VMEM((near_group,) + part, F32),
            pltpu.VMEM((n_ctx, half, poles), F32),
            sem((2,)), sem((2,)),
            sem((near_group,)), sem((near_group,)),
            sem((z_n,)), sem((z_n,)),
            sem((near_group,)), sem((near_group,)),
            sem, sem,
            sem((n_ctx,)), sem((n_ctx,)),
        ],
        compiler_params=pltpu.CompilerParams(
            collective_id=0, has_side_effects=True, vmem_limit_bytes=limit
        ),
        name="chain",
    )(
        states.reshape((cores, 2, near_group) + part),
        near.reshape(cores, half, poles), par.reshape((cores, near_group) + part),
    )

    outs = pl.pallas_call(
        functools.partial(conv_kernel, group, width, poles),
        grid=(steps,),
        in_specs=[big] * 4 + [flat_spec] * 3 + [state_spec],
        out_specs=[big] * 4,
        out_shape=[jax.ShapeDtypeStruct((rows, features), BF16)] * 4,
        compiler_params=pltpu.CompilerParams(vmem_limit_bytes=limit),
        cost_estimate=pl.CostEstimate(
            flops=8 * flops, bytes_accessed=8 * area, transcendentals=0
        ),
        name="convolve",
    )(
        query, key_in, value, cotangent, rates, norm, residues,
        entering.reshape(cores, 2, half, poles, width),
    )
    return (*outs, res.T)


def solution(mesh):
    wide = P(("ctx", "head"), None)
    return jax.shard_map(
        on_device,
        mesh=mesh,
        in_specs=(wide, wide, wide, wide, P(), P()),
        out_specs=(wide, wide, wide, wide, P("head", None)),
        check_vma=False,
    )
```
